256 devices in a mesh: dp: 16 (over z, core), seq: 16 (over y, x).
Axes of the slice: x: 4, y: 4, z: 8, core: 2. Of those that a mesh axis runs over, the one named last changes fastest.
Arguments:
- loader_tokens: bfloat16 [16, 2048, 1408], P('dp', 'seq'), may hold values from -200 to 200
- destination: int32 [16, 2048], P('dp', 'seq'), may hold values from 0 to 32767, as said below
- segment_ids: int32 [16, 2048], P('dp'), may hold values from 0 to 7, as said below
- projection: bfloat16 [1408, 4224], replicated, may hold values from -3 to 3
Outputs:
- mixed_heads: bfloat16 [16, 2048, 1408], P('dp', 'seq')
The draws below stay inside these ranges and needn't reach their ends.
Inputs may be any that keep to these rules, and one draw needn't show every extreme that they name: `destination`: every position of every pack receives exactly one token. A token's position lies in the same block of 128 positions as its own place in the loader's pack. The tokens of one loader pack in one such block go to a pack in numbers 0, 8 or 16, and 16 is reached in every block. `segment_ids`: sample numbers start at 0 in every pack and never fall along it. A sample is an image of 256 tokens or a clip of 512, 1024 or 2048 tokens, beginning at a multiple of its length. Some pack is one clip of 2048 tokens, and some pack holds only images.
All inputs are finite; a program needn't handle non-finite values.
Results may differ from the reference program's by a relative error of at most 0.008.
The reference program's roundings to bfloat16 on the way count: a program that leaves them out, or rounds other values in their place, can miss the bound.
Values may be sent and summed in bfloat16 or wider, within the bound.
A program may use at most 128 MiB of HBM per device.

```python
import jax
import jax.numpy as jnp
from jax import lax

D = 1408
HEADS = 16
HD = 88
TOK_DEV = 128
UNIT = 256
PACK = 2048
N_DP = 16


def draw_loader_tokens(key, part):
    key = jax.random.fold_in(key, 101)
    shape_full = (N_DP, PACK, D)
    result = jax.random.truncated_normal(jax.random.fold_in(key, 4), -6.0, 6.0, shape_full, jnp.float32)
    return result.astype(jnp.bfloat16)


def draw_projection(key, part):
    key = jax.random.fold_in(key, 202)
    shape_full = (D, 3 * D)
    fan_scale = D ** (-0.5)
    result = jax.random.truncated_normal(jax.random.fold_in(key, 4), -6.0, 6.0, shape_full, jnp.float32) * fan_scale
    return result.astype(jnp.bfloat16)


def draw_destination(key, part):
    key = jax.random.fold_in(key, 303)
    pack_count = N_DP
    column_count = PACK // TOK_DEV
    capacity = 2 * TOK_DEV // pack_count
    quarter = pack_count // 4
    pattern = jnp.concatenate([jnp.full((quarter,), capacity, jnp.int32), jnp.full((pack_count // 2,), capacity // 2, jnp.int32), jnp.zeros((pack_count - quarter - pack_count // 2,), jnp.int32)])

    def one_column(column):
        column_key = jax.random.fold_in(key, column)
        shares = pattern[jax.random.permutation(jax.random.fold_in(column_key, 1), pack_count)]
        upper = jnp.cumsum(shares)
        mapping = jax.random.permutation(jax.random.fold_in(column_key, 2), pack_count)
        source_keys = jax.random.split(jax.random.fold_in(column_key, 3), pack_count)
        ranks = jax.vmap(lambda single: jax.random.permutation(single, TOK_DEV))(source_keys)
        offset = jnp.sum((upper[None, None, :] <= ranks[:, :, None]).astype(jnp.int32), axis=-1)
        sources = jnp.arange(pack_count, dtype=jnp.int32)[:, None]
        target = mapping[(sources + offset) % pack_count]
        place_keys = jax.random.split(jax.random.fold_in(column_key, 4), pack_count)
        places = jax.vmap(lambda single: jax.random.permutation(single, TOK_DEV))(place_keys)
        position = places[target, ranks]
        return target * PACK + column * TOK_DEV + position
    blocks_all = jax.vmap(one_column)(jnp.arange(column_count, dtype=jnp.int32))
    return blocks_all.transpose(1, 0, 2).reshape(pack_count, PACK).astype(jnp.int32)


def draw_segment_ids(key, part):
    key = jax.random.fold_in(key, 404)
    pack_count = N_DP
    unit_count = PACK // UNIT
    quarter = unit_count // 4
    pack_index = jnp.arange(pack_count, dtype=jnp.int32)
    chosen = jax.random.randint(jax.random.fold_in(key, 1), (), 0, pack_count)
    images_pack = (chosen + 1 + jax.random.randint(jax.random.fold_in(key, 2), (), 0, pack_count - 1)) % pack_count
    single_clip = (jax.random.randint(jax.random.fold_in(key, 3), (pack_count,), 0, 4) == 0) | (pack_index == chosen)
    single_clip = single_clip & (pack_index != images_pack)
    halves = (jax.random.randint(jax.random.fold_in(key, 4), (pack_count, 2), 0, 2) == 1) & (~single_clip)[:, None]
    halves = halves | (pack_index == images_pack)[:, None]
    images = (jax.random.randint(jax.random.fold_in(key, 5), (pack_count, 4), 0, 2) == 1) & halves[:, jnp.array([0, 0, 1, 1])]
    images = images | (pack_index == images_pack)[:, None]
    unit_index = jnp.arange(unit_count, dtype=jnp.int32)
    starts = (unit_index == 0)[None, :] | (unit_index == unit_count // 2)[None, :] & (~single_clip)[:, None]
    starts = starts | (unit_index % quarter == 0)[None, :] & halves[:, unit_index // (unit_count // 2)]
    starts = starts | images[:, unit_index // quarter]
    numbers = jnp.cumsum(starts.astype(jnp.int32), axis=1) - 1
    return jnp.repeat(numbers, UNIT, axis=1).astype(jnp.int32)


def setup_inputs(seed: int = 0) -> dict:
    arg_keys = jax.random.split(jax.random.key(seed), 5)
    return {
        "loader_tokens": draw_loader_tokens(jax.random.fold_in(arg_keys[4], 71), 0),
        "destination": draw_destination(jax.random.fold_in(arg_keys[4], 71), 0),
        "segment_ids": draw_segment_ids(jax.random.fold_in(arg_keys[4], 71), 0),
        "projection": draw_projection(jax.random.fold_in(arg_keys[4], 71), 0),
    }


MASKED_SCORE = -1e+30
EPSILON = 1e-06

def normalize(rows):
    widened = rows.astype(jnp.float32)
    center = lax.optimization_barrier(jnp.mean(widened, axis=-1, keepdims=True))
    spread = lax.optimization_barrier(jnp.mean(jnp.square(widened - center), axis=-1, keepdims=True))
    return ((widened - center) * lax.rsqrt(spread + EPSILON)).astype(jnp.bfloat16)

def attend(query_head, key_head, value_head, allowed):
    scores = jnp.dot(query_head, key_head.T, preferred_element_type=jnp.float32) * HD ** (-0.5)
    scores = jnp.where(allowed, scores, MASKED_SCORE)
    peak = lax.optimization_barrier(jnp.max(scores, axis=1, keepdims=True))
    weights = jnp.where(allowed, jnp.exp(scores - peak), 0.0)
    totals = lax.optimization_barrier(jnp.sum(weights, axis=1, keepdims=True))
    return jnp.dot(weights.astype(jnp.bfloat16), value_head, preferred_element_type=jnp.float32) / totals

def split_heads(block_data):
    return block_data.reshape(PACK, HEADS, HD).transpose(1, 0, 2)

def reference(loader_tokens, destination, segment_ids, projection):
    flat_rows = loader_tokens.reshape(N_DP * PACK, D)
    packed = jnp.zeros_like(flat_rows).at[destination.reshape(-1)].set(flat_rows).reshape(N_DP, PACK, D)

    def one_pack(operands):
        pack_rows, pack_segment = operands
        projected = jnp.dot(normalize(pack_rows), projection, preferred_element_type=jnp.float32).astype(jnp.bfloat16)
        allowed = pack_segment[:, None] == pack_segment[None, :]
        stacked = (split_heads(projected[:, :D]), split_heads(projected[:, D:2 * D]), split_heads(projected[:, 2 * D:]))
        mixed = lax.map(lambda triple: attend(triple[0], triple[1], triple[2], allowed), stacked)
        return mixed.transpose(1, 0, 2).reshape(PACK, D).astype(jnp.bfloat16)
    return lax.map(one_pack, (packed, segment_ids))
```

```python
import functools
import math

import jax
import jax.numpy as jnp
from jax import lax
from jax.experimental import pallas as pl
from jax.experimental.pallas import tpu as pltpu
from jax.sharding import PartitionSpec as P

HD = 88
UNIT = 256
EPSILON = 1e-06
MASKED_SCORE = -1e30
MESH = pl.DeviceIdType.MESH
F32, BF16, I32 = jnp.float32, jnp.bfloat16, jnp.int32


def iota(shape, dim):
    return lax.broadcasted_iota(I32, shape, dim)


def dot(a, b):
    return jnp.dot(a, b, preferred_element_type=F32)


def ring_order(size):
    return sorted(range(1, size), key=lambda d: -min(d, size - d))


def kernel(
    n_dp, n_seq, tok, dest, seg, w_hbm, out,
    w, sendx, recvx, dests, y_t, sendkv, recvkv, sendq, recvq, keys, values_t, scores, sendo, recvo,
    w_sem, d_send, d_recv, x_send, x_recv, kv_send, kv_recv, q_send, q_recv, o_send, o_recv,
):
    rows, width = tok.shape[1:]
    slots = sendx.shape[0] // n_dp
    pack = n_seq * rows
    pair = UNIT // rows
    units = pack // UNIT
    n_z, n_x = n_dp // 2, math.isqrt(n_seq)
    n_y = n_seq // n_x
    dp, me = lax.axis_index("dp"), lax.axis_index("seq")
    z, core = dp // 2, dp % 2
    y_pos, x_pos = me // n_x, me % n_x

    w_copy = pltpu.make_async_copy(w_hbm, w, w_sem)
    w_copy.start()

    dp_peers = [
        (((z + dz) % n_z) * 2 + c) for c in (0, 1) for dz in ring_order(n_z)
    ] + [z * 2 + (1 - core)]
    dist = lambda d, n: min(d, n - d)
    moves = sorted(
        [(a, b) for a in range(n_y) for b in range(n_x) if (a, b) != (0, 0)],
        key=lambda m: -(dist(m[0], n_y) + dist(m[1], n_x)),
    )
    seq_peers = [((y_pos + a) % n_y) * n_x + (x_pos + b) % n_x for a, b in moves]

    barrier = pltpu.get_barrier_semaphore()
    for p in dp_peers:
        pl.semaphore_signal(barrier, inc=1, device_id=(p, me), device_id_type=MESH)
    for s in seq_peers:
        pl.semaphore_signal(barrier, inc=1, device_id=(dp, s), device_id_type=MESH)

    shift = pack.bit_length() - 1
    own_dest = dest[...]
    dests[dp] = own_dest
    widened = tok[0].astype(F32)
    center = jnp.mean(widened, axis=-1, keepdims=True)
    spread = jnp.mean(jnp.square(widened - center), axis=-1, keepdims=True)
    normed = ((widened - center) * lax.rsqrt(spread + EPSILON)).astype(BF16)
    earlier = (iota((rows, rows), 0) < iota((rows, rows), 1)).astype(F32).astype(BF16)
    own_pack = lax.shift_right_logical(own_dest, shift)
    member = (iota((n_dp, rows), 0) == own_pack).astype(F32)
    rank = jnp.sum(member * dot(member.astype(BF16), earlier), axis=0, keepdims=True)
    slot = own_pack * slots + rank.astype(I32)
    pick = (iota((n_dp * slots, rows), 0) == slot).astype(F32).astype(BF16)
    sendx[...] = dot(pick, normed).astype(BF16)

    pl.semaphore_wait(barrier, len(dp_peers) + len(seq_peers))

    def dest_copy(p, slot_of):
        return pltpu.make_async_remote_copy(
            dest, dests.at[slot_of], d_send.at[p], d_recv.at[slot_of],
            device_id=(p, me), device_id_type=MESH,
        )

    def x_copy(p, slot_of):
        return pltpu.make_async_remote_copy(
            sendx.at[pl.ds(pl.multiple_of(p * slots, slots), slots)],
            recvx.at[pl.ds(pl.multiple_of(slot_of * slots, slots), slots)],
            x_send.at[p], x_recv.at[slot_of],
            device_id=(p, me), device_id_type=MESH,
        )

    def seq_copy(src, dst, send, recv, s, slot_of):
        return pltpu.make_async_remote_copy(
            src.at[s], dst.at[slot_of], send.at[s], recv.at[slot_of],
            device_id=(dp, s), device_id_type=MESH,
        )

    for p in dp_peers:
        dest_copy(p, dp).start()
    for p in dp_peers:
        x_copy(p, dp).start()
    own = pl.ds(pl.multiple_of(dp * slots, slots), slots)
    recvx[own, :] = sendx[own, :]

    for p in dp_peers:
        dest_copy(p, p).wait_recv()
    all_dest = jnp.concatenate([dests[i] for i in range(n_dp)], axis=0)
    here = (lax.shift_right_logical(all_dest, shift) == dp).astype(F32)
    ranks = dot(here.astype(BF16), earlier).astype(I32)
    place = (all_dest & (pack - 1)) - me * rows
    pieces = []
    for i in range(n_dp):
        by_slot = jnp.where(
            iota((slots, rows), 0) == ranks[i : i + 1, :], here[i : i + 1, :], 0.0
        ).astype(BF16)
        by_place = (iota((rows, rows), 0) == place[i : i + 1, :]).astype(F32).astype(BF16)
        pieces.append(
            lax.dot_general(
                by_slot, by_place, (((1,), (1,)), ((), ())), preferred_element_type=F32
            )
        )
    unsort = jnp.concatenate(pieces, axis=0).T.astype(BF16)

    w_copy.wait()
    for p in dp_peers:
        x_copy(p, p).wait_recv()
    x = dot(unsort, recvx[...]).astype(BF16)

    def project(begin, end):
        for c0 in range(begin, end, 256):
            c1 = min(c0 + 256, end)
            y_t[c0:c1, :] = dot(x, w[:, c0:c1]).T

    def kv_of(s):
        k = y_t[pl.ds(pl.multiple_of(width + s * HD, 8), HD), :]
        v = y_t[pl.ds(pl.multiple_of(2 * width + s * HD, 8), HD), :]
        return jnp.concatenate([k, v], axis=0).astype(BF16)

    pad = jnp.zeros((8, rows), F32)

    def q_of(s):
        q = y_t[pl.ds(pl.multiple_of(s * HD, 8), HD), :]
        return jnp.concatenate([q, pad], axis=0).astype(BF16)

    project(width, 3 * width)
    for s in seq_peers:
        sendkv[s] = kv_of(s)
        seq_copy(sendkv, recvkv, kv_send, kv_recv, s, me).start()
    recvkv[me] = kv_of(me)
    project(0, width)
    for s in seq_peers:
        sendq[s] = q_of(s)
        seq_copy(sendq, recvq, q_send, q_recv, s, me).start()
    recvq[me] = q_of(me)

    def unpack(s):
        block = recvkv[s].astype(F32)
        k = jnp.concatenate([block[:HD], jnp.zeros((rows - HD, rows), F32)], axis=0)
        at = pl.ds(pl.multiple_of(s * rows, rows), rows)
        keys[at, :] = k.T.astype(BF16)
        values_t[:, at] = jnp.concatenate([block[HD:], pad], axis=0).astype(BF16)

    unpack(me)
    for s in seq_peers[::-1]:
        seq_copy(sendkv, recvkv, kv_send, kv_recv, s, s).wait_recv()
        unpack(s)

    factor = HD ** (-0.5) * math.log2(math.e)
    filler = jnp.zeros((keys.shape[1] - sendq.shape[1], UNIT), BF16)

    def attend(j):
        q = jnp.concatenate([recvq[j * pair + i] for i in range(pair)], axis=1)
        q = jnp.concatenate([q, filler], axis=0)
        q_seg = seg[:, pl.ds(pl.multiple_of(j * UNIT, UNIT), UNIT)]
        peak = jnp.full((1, UNIT), MASKED_SCORE, F32)
        same = []
        for u in range(units):
            span = slice(u * UNIT, (u + 1) * UNIT)
            part = dot(keys[span, :], q)
            scores[span, :] = part
            same.append(seg[:, span] == q_seg)
            peak = jnp.where(
                same[u], jnp.maximum(peak, jnp.max(part, axis=0, keepdims=True)), peak
            )
        totals = jnp.zeros((1, UNIT), F32)
        mixed = jnp.zeros((values_t.shape[0], UNIT), F32)
        for u in range(units):
            span = slice(u * UNIT, (u + 1) * UNIT)
            level = jnp.where(same[u], peak, -MASKED_SCORE)
            weights = jnp.exp2((scores[span, :] - level) * factor)
            totals += jnp.sum(weights, axis=0, keepdims=True)
            mixed += dot(values_t[:, span], weights.astype(BF16))
        return (mixed / totals).astype(BF16)

    own_j = me // pair

    @pl.loop(1, units)
    def _(k):
        j = (own_j + k) % units
        for i in range(pair):
            s = j * pair + i
            seq_copy(sendq, recvq, q_send, q_recv, s, s).wait_recv()
        mixed = attend(j)
        for i in range(pair):
            s = j * pair + i
            sendo[s] = mixed[:, i * rows : (i + 1) * rows]
            seq_copy(sendo, recvo, o_send, o_recv, s, me).start()

    for i in range(1, pair):
        s = own_j * pair + (me + i) % pair
        seq_copy(sendq, recvq, q_send, q_recv, s, s).wait_recv()
    mixed = attend(own_j)
    for i in range(pair):
        sendo[own_j * pair + i] = mixed[:, i * rows : (i + 1) * rows]
    recvo[me] = sendo[me]
    for i in range(1, pair):
        s = own_j * pair + (me + i) % pair
        seq_copy(sendo, recvo, o_send, o_recv, s, me).start()

    for s in seq_peers:
        seq_copy(sendo, recvo, o_send, o_recv, s, s).wait_recv()
    for h in range(n_seq):
        y_t[h * HD : (h + 1) * HD, :] = recvo[h].astype(F32)[:HD]
    for c0 in range(0, width, 128):
        c1 = min(c0 + 128, width)
        out[0, :, c0:c1] = y_t[c0:c1, :].T.astype(BF16)

    for p in dp_peers:
        dest_copy(p, dp).wait_send()
        x_copy(p, dp).wait_send()
    for s in seq_peers:
        seq_copy(sendkv, recvkv, kv_send, kv_recv, s, me).wait_send()
        seq_copy(sendq, recvq, q_send, q_recv, s, me).wait_send()
        seq_copy(sendo, recvo, o_send, o_recv, s, me).wait_send()


def per_device(n_dp, n_seq, tok, dest, seg, projection):
    rows, width = tok.shape[1:]
    slots = 2 * rows // n_dp
    pack = n_seq * rows
    dma = pltpu.SemaphoreType.DMA
    vmem = pl.BlockSpec(memory_space=pltpu.VMEM)
    return pl.pallas_call(
        functools.partial(kernel, n_dp, n_seq),
        out_shape=jax.ShapeDtypeStruct(tok.shape, BF16),
        in_specs=[vmem, vmem, vmem, pl.BlockSpec(memory_space=pl.ANY)],
        out_specs=vmem,
        scratch_shapes=[
            pltpu.VMEM(projection.shape, BF16),
            pltpu.VMEM((n_dp * slots, width), BF16),
            pltpu.VMEM((n_dp * slots, width), BF16),
            pltpu.VMEM((n_dp, 1, rows), I32),
            pltpu.VMEM((3 * width, rows), F32),
            pltpu.VMEM((n_seq, 2 * HD, rows), BF16),
            pltpu.VMEM((n_seq, 2 * HD, rows), BF16),
            pltpu.VMEM((n_seq, HD + 8, rows), BF16),
            pltpu.VMEM((n_seq, HD + 8, rows), BF16),
            pltpu.VMEM((pack, 128), BF16),
            pltpu.VMEM((HD + 8, pack), BF16),
            pltpu.VMEM((pack, UNIT), F32),
            pltpu.VMEM((n_seq, HD + 8, rows), BF16),
            pltpu.VMEM((n_seq, HD + 8, rows), BF16),
            dma,
        ]
        + [dma((n_dp,))] * 4
        + [dma((n_seq,))] * 6,
        compiler_params=pltpu.CompilerParams(
            collective_id=0, has_side_effects=True, vmem_limit_bytes=56 * 2**20
        ),
    )(tok, dest, seg, projection)


def solution(mesh):
    placed = (P("dp", "seq", None), P("dp", "seq"), P("dp", None), P())
    return jax.shard_map(
        functools.partial(per_device, mesh.shape["dp"], mesh.shape["seq"]),
        mesh=mesh,
        in_specs=placed,
        out_specs=P("dp", "seq", None),
        check_vma=False,
    )
```

```python
import functools
import math

import jax
import jax.numpy as jnp
from jax import lax
from jax.experimental import pallas as pl
from jax.experimental.pallas import tpu as pltpu
from jax.sharding import PartitionSpec as P

HD = 88
UNIT = 256
EPSILON = 1e-06
MASKED_SCORE = -1e30
MESH = pl.DeviceIdType.MESH
F32, BF16, I32 = jnp.float32, jnp.bfloat16, jnp.int32


def iota(shape, dim):
    return lax.broadcasted_iota(I32, shape, dim)


def dot(a, b):
    return jnp.dot(a, b, preferred_element_type=F32)


def ring_order(size):
    return sorted(range(1, size), key=lambda d: -min(d, size - d))


def kernel(
    n_dp, n_seq, tok_hbm, dest_hbm, seg_hbm, w_hbm, heads_out,
    tok, seg, w, sendx, recvx, dests, y_t, sendkv, recvkv, sendq, recvq, keys, values_t, scores_a, scores_b, sendo,
    in_sem, d_send, d_recv, x_send, x_recv, kv_send, kv_recv, q_send, q_recv, o_send, o_recv,
):
    rows, width = tok.shape
    slots = sendx.shape[0] // n_dp
    pack = n_seq * rows
    pair = UNIT // rows
    units = pack // UNIT
    n_z, n_x = n_dp // 2, math.isqrt(n_seq)
    n_y = n_seq // n_x
    dp, me = lax.axis_index("dp"), lax.axis_index("seq")
    z, core = dp // 2, dp % 2
    y_pos, x_pos = me // n_x, me % n_x

    tok_copy = pltpu.make_async_copy(tok_hbm.at[0], tok, in_sem.at[0])
    dest_copy_in = pltpu.make_async_copy(dest_hbm, dests.at[dp], in_sem.at[1])
    seg_copy = pltpu.make_async_copy(seg_hbm, seg, in_sem.at[2])
    w_copy = pltpu.make_async_copy(w_hbm, w, in_sem.at[3])
    tok_copy.start()
    dest_copy_in.start()

    dp_peers = [
        (((z + dz) % n_z) * 2 + c) for c in (0, 1) for dz in ring_order(n_z)
    ] + [z * 2 + (1 - core)]
    dist = lambda d, n: min(d, n - d)
    moves = sorted(
        [(a, b) for a in range(n_y) for b in range(n_x) if (a, b) != (0, 0)],
        key=lambda m: -(dist(m[0], n_y) + dist(m[1], n_x)),
    )
    seq_peers = [((y_pos + a) % n_y) * n_x + (x_pos + b) % n_x for a, b in moves]

    barrier = pltpu.get_barrier_semaphore()
    for p in dp_peers:
        pl.semaphore_signal(barrier, inc=1, device_id=(p, me), device_id_type=MESH)
    for s in seq_peers:
        pl.semaphore_signal(barrier, inc=1, device_id=(dp, s), device_id_type=MESH)

    seg_copy.start()
    w_copy.start()

    shift = pack.bit_length() - 1
    dest_copy_in.wait()
    own_dest = dests[dp]
    tok_copy.wait()
    widened = tok[...].astype(F32)
    center = jnp.mean(widened, axis=-1, keepdims=True)
    spread = jnp.mean(jnp.square(widened - center), axis=-1, keepdims=True)
    normed = ((widened - center) * lax.rsqrt(spread + EPSILON)).astype(BF16)
    earlier = (iota((rows, rows), 0) < iota((rows, rows), 1)).astype(F32).astype(BF16)
    own_pack = lax.shift_right_logical(own_dest, shift)
    member = (iota((n_dp, rows), 0) == own_pack).astype(F32)
    rank = jnp.sum(member * dot(member.astype(BF16), earlier), axis=0, keepdims=True)
    slot = own_pack * slots + rank.astype(I32)
    pick = (iota((n_dp * slots, rows), 0) == slot).astype(F32).astype(BF16)
    sendx[...] = dot(pick, normed).astype(BF16)

    pl.semaphore_wait(barrier, len(dp_peers) + len(seq_peers))

    def dest_copy(p, slot_of):
        return pltpu.make_async_remote_copy(
            dests.at[dp], dests.at[slot_of], d_send, d_recv,
            device_id=(p, me), device_id_type=MESH,
        )

    def x_copy(p, slot_of):
        return pltpu.make_async_remote_copy(
            sendx.at[pl.ds(pl.multiple_of(p * slots, slots), slots)],
            recvx.at[pl.ds(pl.multiple_of(slot_of * slots, slots), slots)],
            x_send, x_recv,
            device_id=(p, me), device_id_type=MESH,
        )

    def seq_copy(src, dst, send, recv, s, slot_of):
        return pltpu.make_async_remote_copy(
            src.at[s], dst.at[slot_of], send, recv,
            device_id=(dp, s), device_id_type=MESH,
        )

    def wait_bytes(ref, count, sem):
        pltpu.make_async_copy(ref.at[pl.ds(0, count)], ref.at[pl.ds(0, count)], sem).wait()

    for p in dp_peers[:2]:
        x_copy(p, dp).start()
    for p in dp_peers[:2]:
        dest_copy(p, dp).start()
    for p in dp_peers[2:]:
        x_copy(p, dp).start()
        dest_copy(p, dp).start()
    own = pl.ds(pl.multiple_of(dp * slots, slots), slots)
    recvx[own, :] = sendx[own, :]

    wait_bytes(dests, n_dp - 1, d_recv)
    all_dest = jnp.concatenate([dests[i] for i in range(n_dp)], axis=0)
    here = (lax.shift_right_logical(all_dest, shift) == dp).astype(F32)
    ranks = dot(here.astype(BF16), earlier).astype(I32)
    place = (all_dest & (pack - 1)) - me * rows
    pieces = []
    for i in range(n_dp):
        by_slot = jnp.where(
            iota((slots, rows), 0) == ranks[i : i + 1, :], here[i : i + 1, :], 0.0
        ).astype(BF16)
        by_place = (iota((rows, rows), 0) == place[i : i + 1, :]).astype(F32).astype(BF16)
        pieces.append(
            lax.dot_general(
                by_slot, by_place, (((1,), (1,)), ((), ())), preferred_element_type=F32
            )
        )
    unsort = jnp.concatenate(pieces, axis=0).T.astype(BF16)

    w_copy.wait()
    wait_bytes(recvx, (n_dp - 1) * slots, x_recv)
    x = dot(unsort, recvx[...]).astype(BF16)

    def project(begin, end):
        for c0 in range(begin, end, 256):
            c1 = min(c0 + 256, end)
            y_t[c0:c1, :] = dot(x, w[:, c0:c1]).T

    def kv_of(s):
        k = y_t[pl.ds(pl.multiple_of(width + s * HD, 8), HD), :]
        v = y_t[pl.ds(pl.multiple_of(2 * width + s * HD, 8), HD), :]
        return jnp.concatenate([k, v], axis=0).astype(BF16)

    pad = jnp.zeros((8, rows), F32)

    def q_of(s):
        q = y_t[pl.ds(pl.multiple_of(s * HD, 8), HD), :]
        return jnp.concatenate([q, pad], axis=0).astype(BF16)

    project(width, 3 * width)
    for s in seq_peers:
        sendkv[s] = kv_of(s)
        seq_copy(sendkv, recvkv, kv_send, kv_recv.at[me], s, me).start()
    recvkv[me] = kv_of(me)
    project(0, width)
    for s in seq_peers:
        sendq[s] = q_of(s)
        seq_copy(sendq, recvq, q_send, q_recv.at[me // pair], s, me).start()
    recvq[me] = q_of(me)

    def unpack(s):
        block = recvkv[s].astype(F32)
        k = jnp.concatenate([block[:HD], jnp.zeros((rows - HD, rows), F32)], axis=0)
        at = pl.ds(pl.multiple_of(s * rows, rows), rows)
        keys[at, :] = k.T.astype(BF16)
        values_t[:, at] = jnp.concatenate([block[HD:], pad], axis=0).astype(BF16)

    unpack(me)
    seg_copy.wait()
    for s in seq_peers:
        seq_copy(sendkv, recvkv, kv_send, kv_recv.at[s], s, s).wait_recv()
        unpack(s)

    factor = HD ** (-0.5) * math.log2(math.e)
    filler = jnp.zeros((keys.shape[1] - sendq.shape[1], UNIT), BF16)
    chunk = min(4, units)

    def spans(g):
        return slice(g * chunk * UNIT, (g + 1) * chunk * UNIT)

    def load(j, count):
        wait_bytes(recvq, count, q_recv.at[j])
        q = jnp.concatenate([recvq[j * pair + i] for i in range(pair)], axis=1)
        q_seg = seg[:, pl.ds(pl.multiple_of(j * UNIT, UNIT), UNIT)]
        same = [seg[:, u * UNIT : (u + 1) * UNIT] == q_seg for u in range(units)]
        return jnp.concatenate([q, filler], axis=0), same

    def score(g, q, same, peak, held):
        part = dot(keys[spans(g), :], q)
        held[spans(g), :] = part
        for i in range(chunk):
            top = jnp.max(part[i * UNIT : (i + 1) * UNIT], axis=0, keepdims=True)
            peak = jnp.where(same[g * chunk + i], jnp.maximum(peak, top), peak)
        return peak

    def mix(g, same, peak, held, totals, mixed):
        pieces = []
        for u in range(g * chunk, (g + 1) * chunk):
            level = jnp.where(same[u], peak, -MASKED_SCORE)
            piece = jnp.exp2((held[u * UNIT : (u + 1) * UNIT, :] - level) * factor)
            totals = totals + jnp.sum(piece.reshape(UNIT // 8, 8, UNIT), axis=0)
            pieces.append(piece.astype(BF16))
        weights = jnp.concatenate(pieces, axis=0)
        return totals, mixed + dot(values_t[:, spans(g)], weights)

    own_j = me // pair
    order = [(own_j + 1 + k) % units for k in range(units)]
    held = (scores_a, scores_b)
    floor = jnp.full((1, UNIT), MASKED_SCORE, F32)
    q, same = load(order[0], pair)
    peak = floor
    for g in range(units // chunk):
        peak = score(g, q, same, peak, held[0])
    for k in range(units):
        now_same, now_peak = same, peak
        last = k == units - 1
        if not last:
            q, same = load(order[k + 1], pair - 1 if k + 1 == units - 1 else pair)
            peak = floor
        totals = jnp.zeros((8, UNIT), F32)
        mixed = jnp.zeros((values_t.shape[0], UNIT), F32)
        for g in range(units // chunk):
            if not last:
                peak = score(g, q, same, peak, held[(k + 1) % 2])
            totals, mixed = mix(g, now_same, now_peak, held[k % 2], totals, mixed)
        result = (mixed / jnp.sum(totals, axis=0, keepdims=True)).astype(BF16)
        for i in range(pair):
            sendo[order[k] * pair + i] = result[:, i * rows : (i + 1) * rows]
        for i in range(1 if last else 0, pair):
            s = own_j * pair + (me + i) % pair if last else order[k] * pair + i
            seq_copy(sendo, heads_out, o_send, o_recv, s, me).start()
    own_copy = pltpu.make_async_copy(sendo.at[me], heads_out.at[me], in_sem.at[4])
    own_copy.start()

    wait_bytes(dests, n_dp - 1, d_send)
    wait_bytes(sendx, (n_dp - 1) * slots, x_send)
    wait_bytes(sendkv, n_seq - 1, kv_send)
    wait_bytes(sendq, n_seq - 1, q_send)
    own_copy.wait()
    wait_bytes(sendo, n_seq - 1, o_send)
    wait_bytes(heads_out, n_seq - 1, o_recv)


def assemble(heads, out, stacked):
    for h in range(heads.shape[0]):
        stacked[h * HD : (h + 1) * HD, :] = heads[h].astype(F32)[:HD]
    width = out.shape[2]
    for c0 in range(0, width, 128):
        c1 = min(c0 + 128, width)
        out[0, :, c0:c1] = stacked[c0:c1, :].T.astype(BF16)


def per_device(n_dp, n_seq, tok, dest, seg, projection):
    rows, width = tok.shape[1:]
    slots = 2 * rows // n_dp
    pack = n_seq * rows
    dma = pltpu.SemaphoreType.DMA
    vmem = pl.BlockSpec(memory_space=pltpu.VMEM)
    anywhere = pl.BlockSpec(memory_space=pl.ANY)
    heads = pl.pallas_call(
        functools.partial(kernel, n_dp, n_seq),
        out_shape=jax.ShapeDtypeStruct((n_seq, HD + 8, rows), BF16),
        in_specs=[anywhere] * 4,
        out_specs=anywhere,
        scratch_shapes=[
            pltpu.VMEM((rows, width), BF16),
            pltpu.VMEM(seg.shape, I32),
            pltpu.VMEM(projection.shape, BF16),
            pltpu.VMEM((n_dp * slots, width), BF16),
            pltpu.VMEM((n_dp * slots, width), BF16),
            pltpu.VMEM((n_dp, 1, rows), I32),
            pltpu.VMEM((3 * width, rows), F32),
            pltpu.VMEM((n_seq, 2 * HD, rows), BF16),
            pltpu.VMEM((n_seq, 2 * HD, rows), BF16),
            pltpu.VMEM((n_seq, HD + 8, rows), BF16),
            pltpu.VMEM((n_seq, HD + 8, rows), BF16),
            pltpu.VMEM((pack, 128), BF16),
            pltpu.VMEM((HD + 8, pack), BF16),
            pltpu.VMEM((pack, UNIT), F32),
            pltpu.VMEM((pack, UNIT), F32),
            pltpu.VMEM((n_seq, HD + 8, rows), BF16),
            dma((5,)),
            dma,
            dma,
            dma,
            dma,
            dma,
            dma((n_seq,)),
            dma,
            dma((pack // UNIT,)),
            dma,
            dma,
        ],
        compiler_params=pltpu.CompilerParams(
            collective_id=0, has_side_effects=True, vmem_limit_bytes=56 * 2**20
        ),
    )(tok, dest, seg, projection)
    return pl.pallas_call(
        assemble,
        out_shape=jax.ShapeDtypeStruct(tok.shape, BF16),
        in_specs=[vmem],
        out_specs=vmem,
        scratch_shapes=[pltpu.VMEM((width, rows), F32)],
        compiler_params=pltpu.CompilerParams(vmem_limit_bytes=32 * 2**20),
    )(heads)


def solution(mesh):
    placed = (P("dp", "seq", None), P("dp", "seq"), P("dp", None), P())
    return jax.shard_map(
        functools.partial(per_device, mesh.shape["dp"], mesh.shape["seq"]),
        mesh=mesh,
        in_specs=placed,
        out_specs=P("dp", "seq", None),
        check_vma=False,
    )
```

```python
import functools
import math

import jax
import jax.numpy as jnp
from jax import lax
from jax.experimental import pallas as pl
from jax.experimental.pallas import tpu as pltpu
from jax.sharding import PartitionSpec as P

HD = 88
UNIT = 256
EPSILON = 1e-06
MASKED_SCORE = -1e30
MESH = pl.DeviceIdType.MESH
F32, BF16, I32 = jnp.float32, jnp.bfloat16, jnp.int32


def iota(shape, dim):
    return lax.broadcasted_iota(I32, shape, dim)


def dot(a, b):
    return jnp.dot(a, b, preferred_element_type=F32)


def ring_order(size):
    return sorted(range(1, size), key=lambda d: -min(d, size - d))


def kernel(
    n_dp, n_seq, tok_hbm, dest_hbm, seg_hbm, w_hbm, heads_out,
    tok, seg, w, sendx, recvx, dests, y_t, sendkv, recvkv, sendq, recvq, keys, values_t, scores_a, scores_b, sendo,
    in_sem, d_send, d_recv, x_send, x_recv, kv_send, kv_recv, q_send, q_recv, o_send, o_recv,
):
    rows, width = tok.shape
    slots = sendx.shape[0] // n_dp
    pack = n_seq * rows
    pair = UNIT // rows
    units = pack // UNIT
    n_z, n_x = n_dp // 2, math.isqrt(n_seq)
    n_y = n_seq // n_x
    dp, me = lax.axis_index("dp"), lax.axis_index("seq")
    z, core = dp // 2, dp % 2
    y_pos, x_pos = me // n_x, me % n_x

    tok_copy = pltpu.make_async_copy(tok_hbm.at[0], tok, in_sem.at[0])
    dest_copy_in = pltpu.make_async_copy(dest_hbm, dests.at[dp], in_sem.at[1])
    seg_copy = pltpu.make_async_copy(seg_hbm, seg, in_sem.at[2])
    w_copy = pltpu.make_async_copy(w_hbm, w, in_sem.at[3])
    tok_copy.start()
    dest_copy_in.start()

    dp_peers = [
        (((z + dz) % n_z) * 2 + c) for c in (0, 1) for dz in ring_order(n_z)
    ] + [z * 2 + (1 - core)]
    dist = lambda d, n: min(d, n - d)
    moves = sorted(
        [(a, b) for a in range(n_y) for b in range(n_x) if (a, b) != (0, 0)],
        key=lambda m: -(dist(m[0], n_y) + dist(m[1], n_x)),
    )
    seq_peers = [((y_pos + a) % n_y) * n_x + (x_pos + b) % n_x for a, b in moves]

    barrier = pltpu.get_barrier_semaphore()
    for p in dp_peers:
        pl.semaphore_signal(barrier, inc=1, device_id=(p, me), device_id_type=MESH)
    for s in seq_peers:
        pl.semaphore_signal(barrier, inc=1, device_id=(dp, s), device_id_type=MESH)

    seg_copy.start()
    w_copy.start()

    shift = pack.bit_length() - 1
    dest_copy_in.wait()
    own_dest = dests[dp]
    tok_copy.wait()
    widened = tok[...].astype(F32)
    center = jnp.mean(widened, axis=-1, keepdims=True)
    spread = jnp.mean(jnp.square(widened - center), axis=-1, keepdims=True)
    normed = ((widened - center) * lax.rsqrt(spread + EPSILON)).astype(BF16)
    earlier = (iota((rows, rows), 0) < iota((rows, rows), 1)).astype(F32).astype(BF16)
    own_pack = lax.shift_right_logical(own_dest, shift)
    member = (iota((n_dp, rows), 0) == own_pack).astype(F32)
    rank = jnp.sum(member * dot(member.astype(BF16), earlier), axis=0, keepdims=True)
    slot = own_pack * slots + rank.astype(I32)
    pick = (iota((n_dp * slots, rows), 0) == slot).astype(F32).astype(BF16)
    sendx[...] = dot(pick, normed).astype(BF16)

    pl.semaphore_wait(barrier, len(dp_peers) + len(seq_peers))

    def dest_copy(p, slot_of):
        return pltpu.make_async_remote_copy(
            dests.at[dp], dests.at[slot_of], d_send, d_recv,
            device_id=(p, me), device_id_type=MESH,
        )

    def x_copy(p, slot_of):
        return pltpu.make_async_remote_copy(
            sendx.at[pl.ds(pl.multiple_of(p * slots, slots), slots)],
            recvx.at[pl.ds(pl.multiple_of(slot_of * slots, slots), slots)],
            x_send, x_recv,
            device_id=(p, me), device_id_type=MESH,
        )

    def seq_copy(src, dst, send, recv, s, slot_of):
        return pltpu.make_async_remote_copy(
            src.at[s], dst.at[slot_of], send, recv,
            device_id=(dp, s), device_id_type=MESH,
        )

    def wait_bytes(ref, count, sem):
        pltpu.make_async_copy(ref.at[pl.ds(0, count)], ref.at[pl.ds(0, count)], sem).wait()

    for p in dp_peers[:2]:
        x_copy(p, dp).start()
    for p in dp_peers[:2]:
        dest_copy(p, dp).start()
    for p in dp_peers[2:]:
        x_copy(p, dp).start()
        dest_copy(p, dp).start()
    own = pl.ds(pl.multiple_of(dp * slots, slots), slots)
    recvx[own, :] = sendx[own, :]

    wait_bytes(dests, n_dp - 1, d_recv)
    all_dest = jnp.concatenate([dests[i] for i in range(n_dp)], axis=0)
    here = (lax.shift_right_logical(all_dest, shift) == dp).astype(F32)
    ranks = dot(here.astype(BF16), earlier).astype(I32)
    place = (all_dest & (pack - 1)) - me * rows
    pieces = []
    for i in range(n_dp):
        by_slot = jnp.where(
            iota((slots, rows), 0) == ranks[i : i + 1, :], here[i : i + 1, :], 0.0
        ).astype(BF16)
        by_place = (iota((rows, rows), 0) == place[i : i + 1, :]).astype(F32).astype(BF16)
        pieces.append(
            lax.dot_general(
                by_slot, by_place, (((1,), (1,)), ((), ())), preferred_element_type=F32
            )
        )
    unsort = jnp.concatenate(pieces, axis=0).T.astype(BF16)

    w_copy.wait()
    wait_bytes(recvx, (n_dp - 1) * slots, x_recv)
    x = dot(unsort, recvx[...]).astype(BF16)

    def project(begin, end):
        for c0 in range(begin, end, 256):
            c1 = min(c0 + 256, end)
            y_t[c0:c1, :] = dot(x, w[:, c0:c1]).T

    def kv_of(s):
        k = y_t[pl.ds(pl.multiple_of(width + s * HD, 8), HD), :]
        v = y_t[pl.ds(pl.multiple_of(2 * width + s * HD, 8), HD), :]
        return jnp.concatenate([k, v], axis=0).astype(BF16)

    pad = jnp.zeros((8, rows), F32)

    def q_of(s):
        q = y_t[pl.ds(pl.multiple_of(s * HD, 8), HD), :]
        return jnp.concatenate([q, pad], axis=0).astype(BF16)

    project(0, width)
    for s in seq_peers:
        sendq[s] = q_of(s)
        seq_copy(sendq, recvq, q_send, q_recv.at[me // pair], s, me).start()
    recvq[me] = q_of(me)
    project(width, 3 * width)
    for s in seq_peers:
        sendkv[s] = kv_of(s)
        seq_copy(sendkv, recvkv, kv_send, kv_recv.at[me], s, me).start()
    recvkv[me] = kv_of(me)

    def unpack(s):
        block = recvkv[s].astype(F32)
        k = jnp.concatenate([block[:HD], jnp.zeros((rows - HD, rows), F32)], axis=0)
        at = pl.ds(pl.multiple_of(s * rows, rows), rows)
        keys[at, :] = k.T.astype(BF16)
        values_t[:, at] = jnp.concatenate([block[HD:], pad], axis=0).astype(BF16)

    unpack(me)
    seg_copy.wait()
    for s in seq_peers:
        seq_copy(sendkv, recvkv, kv_send, kv_recv.at[s], s, s).wait_recv()
        unpack(s)

    factor = HD ** (-0.5) * math.log2(math.e)
    filler = jnp.zeros((keys.shape[1] - sendq.shape[1], UNIT), BF16)
    chunk = min(4, units)

    def spans(g):
        return slice(g * chunk * UNIT, (g + 1) * chunk * UNIT)

    def load(j, count):
        wait_bytes(recvq, count, q_recv.at[j])
        q = jnp.concatenate([recvq[j * pair + i] for i in range(pair)], axis=1)
        q_seg = seg[:, pl.ds(pl.multiple_of(j * UNIT, UNIT), UNIT)]
        same = [seg[:, u * UNIT : (u + 1) * UNIT] == q_seg for u in range(units)]
        return jnp.concatenate([q, filler], axis=0), same

    def score(g, q, same, peak, held):
        part = dot(keys[spans(g), :], q)
        held[spans(g), :] = part
        for i in range(chunk):
            top = jnp.max(part[i * UNIT : (i + 1) * UNIT], axis=0, keepdims=True)
            peak = jnp.where(same[g * chunk + i], jnp.maximum(peak, top), peak)
        return peak

    def mix(g, same, peak, held, totals, mixed):
        pieces = []
        for u in range(g * chunk, (g + 1) * chunk):
            level = jnp.where(same[u], peak, -MASKED_SCORE)
            piece = jnp.exp2((held[u * UNIT : (u + 1) * UNIT, :] - level) * factor)
            totals = totals + jnp.sum(piece.reshape(UNIT // 8, 8, UNIT), axis=0)
            pieces.append(piece.astype(BF16))
        weights = jnp.concatenate(pieces, axis=0)
        return totals, mixed + dot(values_t[:, spans(g)], weights)

    own_j = me // pair
    order = [(own_j + 1 + k) % units for k in range(units)]
    held = (scores_a, scores_b)
    floor = jnp.full((1, UNIT), MASKED_SCORE, F32)
    q, same = load(order[0], pair)
    peak = floor
    for g in range(units // chunk):
        peak = score(g, q, same, peak, held[0])
    for k in range(units):
        now_same, now_peak = same, peak
        last = k == units - 1
        if not last:
            q, same = load(order[k + 1], pair - 1 if k + 1 == units - 1 else pair)
            peak = floor
        totals = jnp.zeros((8, UNIT), F32)
        mixed = jnp.zeros((values_t.shape[0], UNIT), F32)
        for g in range(units // chunk):
            if not last:
                peak = score(g, q, same, peak, held[(k + 1) % 2])
            totals, mixed = mix(g, now_same, now_peak, held[k % 2], totals, mixed)
        result = (mixed / jnp.sum(totals, axis=0, keepdims=True)).astype(BF16)
        for i in range(pair):
            sendo[order[k] * pair + i] = result[:, i * rows : (i + 1) * rows]
        for i in range(1 if last else 0, pair):
            s = own_j * pair + (me + i) % pair if last else order[k] * pair + i
            seq_copy(sendo, heads_out, o_send, o_recv, s, me).start()
    own_copy = pltpu.make_async_copy(sendo.at[me], heads_out.at[me], in_sem.at[4])
    own_copy.start()

    wait_bytes(dests, n_dp - 1, d_send)
    wait_bytes(sendx, (n_dp - 1) * slots, x_send)
    wait_bytes(sendkv, n_seq - 1, kv_send)
    wait_bytes(sendq, n_seq - 1, q_send)
    own_copy.wait()
    wait_bytes(sendo, n_seq - 1, o_send)
    wait_bytes(heads_out, n_seq - 1, o_recv)


def assemble(heads, out, stacked):
    for h in range(heads.shape[0]):
        stacked[h * HD : (h + 1) * HD, :] = heads[h].astype(F32)[:HD]
    width = out.shape[2]
    for c0 in range(0, width, 128):
        c1 = min(c0 + 128, width)
        out[0, :, c0:c1] = stacked[c0:c1, :].T.astype(BF16)


def per_device(n_dp, n_seq, tok, dest, seg, projection):
    rows, width = tok.shape[1:]
    slots = 2 * rows // n_dp
    pack = n_seq * rows
    dma = pltpu.SemaphoreType.DMA
    vmem = pl.BlockSpec(memory_space=pltpu.VMEM)
    anywhere = pl.BlockSpec(memory_space=pl.ANY)
    heads = pl.pallas_call(
        functools.partial(kernel, n_dp, n_seq),
        out_shape=jax.ShapeDtypeStruct((n_seq, HD + 8, rows), BF16),
        in_specs=[anywhere] * 4,
        out_specs=anywhere,
        scratch_shapes=[
            pltpu.VMEM((rows, width), BF16),
            pltpu.VMEM(seg.shape, I32),
            pltpu.VMEM(projection.shape, BF16),
            pltpu.VMEM((n_dp * slots, width), BF16),
            pltpu.VMEM((n_dp * slots, width), BF16),
            pltpu.VMEM((n_dp, 1, rows), I32),
            pltpu.VMEM((3 * width, rows), F32),
            pltpu.VMEM((n_seq, 2 * HD, rows), BF16),
            pltpu.VMEM((n_seq, 2 * HD, rows), BF16),
            pltpu.VMEM((n_seq, HD + 8, rows), BF16),
            pltpu.VMEM((n_seq, HD + 8, rows), BF16),
            pltpu.VMEM((pack, 128), BF16),
            pltpu.VMEM((HD + 8, pack), BF16),
            pltpu.VMEM((pack, UNIT), F32),
            pltpu.VMEM((pack, UNIT), F32),
            pltpu.VMEM((n_seq, HD + 8, rows), BF16),
            dma((5,)),
            dma,
            dma,
            dma,
            dma,
            dma,
            dma((n_seq,)),
            dma,
            dma((pack // UNIT,)),
            dma,
            dma,
        ],
        compiler_params=pltpu.CompilerParams(
            collective_id=0, has_side_effects=True, vmem_limit_bytes=56 * 2**20
        ),
    )(tok, dest, seg, projection)
    return pl.pallas_call(
        assemble,
        out_shape=jax.ShapeDtypeStruct(tok.shape, BF16),
        in_specs=[vmem],
        out_specs=vmem,
        scratch_shapes=[pltpu.VMEM((width, rows), F32)],
        compiler_params=pltpu.CompilerParams(vmem_limit_bytes=32 * 2**20),
    )(heads)


def solution(mesh):
    placed = (P("dp", "seq", None), P("dp", "seq"), P("dp", None), P())
    return jax.shard_map(
        functools.partial(per_device, mesh.shape["dp"], mesh.shape["seq"]),
        mesh=mesh,
        in_specs=placed,
        out_specs=P("dp", "seq", None),
        check_vma=False,
    )
```

```python
import functools
import math

import jax
import jax.numpy as jnp
from jax import lax
from jax.experimental import pallas as pl
from jax.experimental.pallas import tpu as pltpu
from jax.sharding import PartitionSpec as P

HD = 88
UNIT = 256
EPSILON = 1e-06
MASKED_SCORE = -1e30
MESH = pl.DeviceIdType.MESH
F32, BF16, I32 = jnp.float32, jnp.bfloat16, jnp.int32


def iota(shape, dim):
    return lax.broadcasted_iota(I32, shape, dim)


def dot(a, b):
    return jnp.dot(a, b, preferred_element_type=F32)


def ring_order(size):
    return sorted(range(1, size), key=lambda d: -min(d, size - d))


def kernel(
    n_dp, n_seq, tok_hbm, dest_hbm, seg_hbm, w_hbm, heads_out,
    tok, seg, w, sendx, recvx, dests, y_t, sendkv, recvkv, sendq, recvq, keys, values_t, scores_a, scores_b, sendo,
    in_sem, d_send, d_recv, x_send, x_recv, kv_send, kv_recv, q_send, q_recv, o_send, o_recv,
):
    rows, width = tok.shape
    slots = sendx.shape[0] // n_dp
    pack = n_seq * rows
    pair = UNIT // rows
    units = pack // UNIT
    n_z, n_x = n_dp // 2, math.isqrt(n_seq)
    n_y = n_seq // n_x
    dp, me = lax.axis_index("dp"), lax.axis_index("seq")
    z, core = dp // 2, dp % 2
    y_pos, x_pos = me // n_x, me % n_x

    tok_copy = pltpu.make_async_copy(tok_hbm.at[0], tok, in_sem.at[0])
    dest_copy_in = pltpu.make_async_copy(dest_hbm, dests.at[dp], in_sem.at[1])
    seg_copy = pltpu.make_async_copy(seg_hbm, seg, in_sem.at[2])
    w_copy = pltpu.make_async_copy(w_hbm, w, in_sem.at[3])
    tok_copy.start()
    dest_copy_in.start()

    dp_peers = [z * 2 + (1 - core)] + [
        (((z + dz) % n_z) * 2 + c) for c in (0, 1) for dz in ring_order(n_z)
    ]
    dist = lambda d, n: min(d, n - d)
    moves = sorted(
        [(a, b) for a in range(n_y) for b in range(n_x) if (a, b) != (0, 0)],
        key=lambda m: -(dist(m[0], n_y) + dist(m[1], n_x)),
    )
    seq_peers = [((y_pos + a) % n_y) * n_x + (x_pos + b) % n_x for a, b in moves]

    barrier = pltpu.get_barrier_semaphore()
    for p in dp_peers:
        pl.semaphore_signal(barrier, inc=1, device_id=(p, me), device_id_type=MESH)
    for s in seq_peers:
        pl.semaphore_signal(barrier, inc=1, device_id=(dp, s), device_id_type=MESH)

    seg_copy.start()
    w_copy.start()

    shift = pack.bit_length() - 1
    dest_copy_in.wait()
    own_dest = dests[dp]
    tok_copy.wait()
    widened = tok[...].astype(F32)
    center = jnp.mean(widened, axis=-1, keepdims=True)
    spread = jnp.mean(jnp.square(widened - center), axis=-1, keepdims=True)
    normed = ((widened - center) * lax.rsqrt(spread + EPSILON)).astype(BF16)
    earlier = (iota((rows, rows), 0) < iota((rows, rows), 1)).astype(F32).astype(BF16)
    own_pack = lax.shift_right_logical(own_dest, shift)
    member = (iota((n_dp, rows), 0) == own_pack).astype(F32)
    rank = jnp.sum(member * dot(member.astype(BF16), earlier), axis=0, keepdims=True)
    slot = own_pack * slots + rank.astype(I32)
    pick = (iota((n_dp * slots, rows), 0) == slot).astype(F32).astype(BF16)
    sendx[...] = dot(pick, normed).astype(BF16)

    pl.semaphore_wait(barrier, len(dp_peers) + len(seq_peers))

    def dest_copy(p, slot_of):
        return pltpu.make_async_remote_copy(
            dests.at[dp], dests.at[slot_of], d_send, d_recv,
            device_id=(p, me), device_id_type=MESH,
        )

    def x_copy(p, slot_of, group):
        return pltpu.make_async_remote_copy(
            sendx.at[pl.ds(pl.multiple_of(p * slots, slots), slots)],
            recvx.at[pl.ds(pl.multiple_of(slot_of * slots, slots), slots)],
            x_send.at[group], x_recv,
            device_id=(p, me), device_id_type=MESH,
        )

    def seq_copy(src, dst, send, recv, s, slot_of):
        return pltpu.make_async_remote_copy(
            src.at[s], dst.at[slot_of], send, recv,
            device_id=(dp, s), device_id_type=MESH,
        )

    def wait_bytes(ref, count, sem):
        pltpu.make_async_copy(ref.at[pl.ds(0, count)], ref.at[pl.ds(0, count)], sem).wait()

    for p in dp_peers[0:4]:
        x_copy(p, dp, 0).start()
    for p in dp_peers:
        dest_copy(p, dp).start()
    for p in dp_peers[4:8]:
        x_copy(p, dp, 1).start()
    wait_bytes(sendx, 4 * slots, x_send.at[0])
    for p in dp_peers[8:12]:
        x_copy(p, dp, 2).start()
    wait_bytes(sendx, 4 * slots, x_send.at[1])
    for p in dp_peers[12:15]:
        x_copy(p, dp, 3).start()
    own = pl.ds(pl.multiple_of(dp * slots, slots), slots)
    recvx[own, :] = sendx[own, :]

    wait_bytes(dests, n_dp - 1, d_recv)
    all_dest = jnp.concatenate([dests[i] for i in range(n_dp)], axis=0)
    here = (lax.shift_right_logical(all_dest, shift) == dp).astype(F32)
    ranks = dot(here.astype(BF16), earlier).astype(I32)
    place = (all_dest & (pack - 1)) - me * rows
    pieces = []
    for i in range(n_dp):
        by_slot = jnp.where(
            iota((slots, rows), 0) == ranks[i : i + 1, :], here[i : i + 1, :], 0.0
        ).astype(BF16)
        by_place = (iota((rows, rows), 0) == place[i : i + 1, :]).astype(F32).astype(BF16)
        pieces.append(
            lax.dot_general(
                by_slot, by_place, (((1,), (1,)), ((), ())), preferred_element_type=F32
            )
        )
    unsort = jnp.concatenate(pieces, axis=0).T.astype(BF16)

    w_copy.wait()
    wait_bytes(recvx, (n_dp - 1) * slots, x_recv)
    x = dot(unsort, recvx[...]).astype(BF16)

    def project(begin, end):
        for c0 in range(begin, end, 256):
            c1 = min(c0 + 256, end)
            y_t[c0:c1, :] = dot(x, w[:, c0:c1]).T

    def kv_of(s):
        k = y_t[pl.ds(pl.multiple_of(width + s * HD, 8), HD), :]
        v = y_t[pl.ds(pl.multiple_of(2 * width + s * HD, 8), HD), :]
        return jnp.concatenate([k, v], axis=0).astype(BF16)

    pad = jnp.zeros((8, rows), F32)

    def q_of(s):
        q = y_t[pl.ds(pl.multiple_of(s * HD, 8), HD), :]
        return jnp.concatenate([q, pad], axis=0).astype(BF16)

    project(0, width)
    for s in seq_peers:
        sendq[s] = q_of(s)
        seq_copy(sendq, recvq, q_send, q_recv.at[me // pair], s, me).start()
    recvq[me] = q_of(me)
    project(width, 3 * width)
    for s in seq_peers:
        sendkv[s] = kv_of(s)
        seq_copy(sendkv, recvkv, kv_send, kv_recv.at[me], s, me).start()
    recvkv[me] = kv_of(me)

    def unpack(s):
        block = recvkv[s].astype(F32)
        k = jnp.concatenate([block[:HD], jnp.zeros((rows - HD, rows), F32)], axis=0)
        at = pl.ds(pl.multiple_of(s * rows, rows), rows)
        keys[at, :] = k.T.astype(BF16)
        values_t[:, at] = jnp.concatenate([block[HD:], pad], axis=0).astype(BF16)

    unpack(me)
    seg_copy.wait()
    for s in seq_peers:
        seq_copy(sendkv, recvkv, kv_send, kv_recv.at[s], s, s).wait_recv()
        unpack(s)

    factor = HD ** (-0.5) * math.log2(math.e)
    filler = jnp.zeros((keys.shape[1] - sendq.shape[1], UNIT), BF16)
    chunk = min(8, units)

    def spans(g):
        return slice(g * chunk * UNIT, (g + 1) * chunk * UNIT)

    def load(j, count):
        wait_bytes(recvq, count, q_recv.at[j])
        q = jnp.concatenate([recvq[j * pair + i] for i in range(pair)], axis=1)
        q_seg = seg[:, pl.ds(pl.multiple_of(j * UNIT, UNIT), UNIT)]
        same = [seg[:, u * UNIT : (u + 1) * UNIT] == q_seg for u in range(units)]
        return jnp.concatenate([q, filler], axis=0), same

    def score(g, q, same, peak, held):
        part = dot(keys[spans(g), :], q)
        held[spans(g), :] = part
        for i in range(chunk):
            top = jnp.max(part[i * UNIT : (i + 1) * UNIT], axis=0, keepdims=True)
            peak = jnp.where(same[g * chunk + i], jnp.maximum(peak, top), peak)
        return peak

    def mix(g, same, peak, held, totals, mixed):
        pieces = []
        for u in range(g * chunk, (g + 1) * chunk):
            level = jnp.where(same[u], peak, -MASKED_SCORE)
            piece = jnp.exp2((held[u * UNIT : (u + 1) * UNIT, :] - level) * factor)
            totals = totals + jnp.sum(piece.reshape(UNIT // 8, 8, UNIT), axis=0)
            pieces.append(piece.astype(BF16))
        weights = jnp.concatenate(pieces, axis=0)
        return totals, mixed + dot(values_t[:, spans(g)], weights)

    own_j = me // pair
    order = [(own_j + 1 + k) % units for k in range(units)]
    held = (scores_a, scores_b)
    floor = jnp.full((1, UNIT), MASKED_SCORE, F32)
    q, same = load(order[0], pair)
    peak = floor
    for g in range(units // chunk):
        peak = score(g, q, same, peak, held[0])
    for k in range(units):
        now_same, now_peak = same, peak
        last = k == units - 1
        if not last:
            q, same = load(order[k + 1], pair - 1 if k + 1 == units - 1 else pair)
            peak = floor
        totals = jnp.zeros((8, UNIT), F32)
        mixed = jnp.zeros((values_t.shape[0], UNIT), F32)
        for g in range(units // chunk):
            if not last:
                peak = score(g, q, same, peak, held[(k + 1) % 2])
            totals, mixed = mix(g, now_same, now_peak, held[k % 2], totals, mixed)
        result = (mixed / jnp.sum(totals, axis=0, keepdims=True)).astype(BF16)
        for i in range(pair):
            sendo[order[k] * pair + i] = result[:, i * rows : (i + 1) * rows]
        for i in range(1 if last else 0, pair):
            s = own_j * pair + (me + i) % pair if last else order[k] * pair + i
            seq_copy(sendo, heads_out, o_send, o_recv, s, me).start()
    own_copy = pltpu.make_async_copy(sendo.at[me], heads_out.at[me], in_sem.at[4])
    own_copy.start()

    wait_bytes(dests, n_dp - 1, d_send)
    wait_bytes(sendx, 4 * slots, x_send.at[2])
    wait_bytes(sendx, 3 * slots, x_send.at[3])
    wait_bytes(sendkv, n_seq - 1, kv_send)
    wait_bytes(sendq, n_seq - 1, q_send)
    own_copy.wait()
    wait_bytes(sendo, n_seq - 1, o_send)
    wait_bytes(heads_out, n_seq - 1, o_recv)


def assemble(heads, out, stacked):
    for h in range(heads.shape[0]):
        stacked[h * HD : (h + 1) * HD, :] = heads[h].astype(F32)[:HD]
    width = out.shape[2]
    for c0 in range(0, width, 128):
        c1 = min(c0 + 128, width)
        out[0, :, c0:c1] = stacked[c0:c1, :].T.astype(BF16)


def per_device(n_dp, n_seq, tok, dest, seg, projection):
    rows, width = tok.shape[1:]
    slots = 2 * rows // n_dp
    pack = n_seq * rows
    dma = pltpu.SemaphoreType.DMA
    vmem = pl.BlockSpec(memory_space=pltpu.VMEM)
    anywhere = pl.BlockSpec(memory_space=pl.ANY)
    heads = pl.pallas_call(
        functools.partial(kernel, n_dp, n_seq),
        out_shape=jax.ShapeDtypeStruct((n_seq, HD + 8, rows), BF16),
        in_specs=[anywhere] * 4,
        out_specs=anywhere,
        scratch_shapes=[
            pltpu.VMEM((rows, width), BF16),
            pltpu.VMEM(seg.shape, I32),
            pltpu.VMEM(projection.shape, BF16),
            pltpu.VMEM((n_dp * slots, width), BF16),
            pltpu.VMEM((n_dp * slots, width), BF16),
            pltpu.VMEM((n_dp, 1, rows), I32),
            pltpu.VMEM((3 * width, rows), F32),
            pltpu.VMEM((n_seq, 2 * HD, rows), BF16),
            pltpu.VMEM((n_seq, 2 * HD, rows), BF16),
            pltpu.VMEM((n_seq, HD + 8, rows), BF16),
            pltpu.VMEM((n_seq, HD + 8, rows), BF16),
            pltpu.VMEM((pack, 128), BF16),
            pltpu.VMEM((HD + 8, pack), BF16),
            pltpu.VMEM((pack, UNIT), F32),
            pltpu.VMEM((pack, UNIT), F32),
            pltpu.VMEM((n_seq, HD + 8, rows), BF16),
            dma((5,)),
            dma,
            dma,
            dma((4,)),
            dma,
            dma,
            dma((n_seq,)),
            dma,
            dma((pack // UNIT,)),
            dma,
            dma,
        ],
        compiler_params=pltpu.CompilerParams(
            collective_id=0, has_side_effects=True, vmem_limit_bytes=56 * 2**20
        ),
    )(tok, dest, seg, projection)
    return pl.pallas_call(
        assemble,
        out_shape=jax.ShapeDtypeStruct(tok.shape, BF16),
        in_specs=[vmem],
        out_specs=vmem,
        scratch_shapes=[pltpu.VMEM((width, rows), F32)],
        compiler_params=pltpu.CompilerParams(vmem_limit_bytes=32 * 2**20),
    )(heads)


def solution(mesh):
    placed = (P("dp", "seq", None), P("dp", "seq"), P("dp", None), P())
    return jax.shard_map(
        functools.partial(per_device, mesh.shape["dp"], mesh.shape["seq"]),
        mesh=mesh,
        in_specs=placed,
        out_specs=P("dp", "seq", None),
        check_vma=False,
    )
```

```python
import functools
import math

import jax
import jax.numpy as jnp
from jax import lax
from jax.experimental import pallas as pl
from jax.experimental.pallas import tpu as pltpu
from jax.sharding import PartitionSpec as P

HD = 88
UNIT = 256
EPSILON = 1e-06
MASKED_SCORE = -1e30
MESH = pl.DeviceIdType.MESH
F32, BF16, I32 = jnp.float32, jnp.bfloat16, jnp.int32


def iota(shape, dim):
    return lax.broadcasted_iota(I32, shape, dim)


def dot(a, b):
    return jnp.dot(a, b, preferred_element_type=F32)


def ring_order(size):
    return sorted(range(1, size), key=lambda d: -min(d, size - d))


def kernel(
    n_dp, n_seq, tok_hbm, dest_hbm, seg_hbm, w_hbm, heads_out,
    tok, seg, w, sendx, recvx, dests, y_t, sendkv, recvkv, sendq, recvq, keys, values_t, scores_a, scores_b, sendo,
    in_sem, d_send, d_recv, x_send, x_recv, kv_send, kv_recv, q_send, q_recv, o_send, o_recv,
):
    rows, width = tok.shape
    slots = sendx.shape[0] // n_dp
    pack = n_seq * rows
    pair = UNIT // rows
    units = pack // UNIT
    n_z, n_x = n_dp // 2, math.isqrt(n_seq)
    n_y = n_seq // n_x
    dp, me = lax.axis_index("dp"), lax.axis_index("seq")
    z, core = dp // 2, dp % 2
    y_pos, x_pos = me // n_x, me % n_x

    tok_copy = pltpu.make_async_copy(tok_hbm.at[0], tok, in_sem.at[0])
    dest_copy_in = pltpu.make_async_copy(dest_hbm, dests.at[dp], in_sem.at[1])
    seg_copy = pltpu.make_async_copy(seg_hbm, seg, in_sem.at[2])
    w_copy = pltpu.make_async_copy(w_hbm, w, in_sem.at[3])
    tok_copy.start()
    dest_copy_in.start()

    dp_peers = [z * 2 + (1 - core)] + [
        (((z + dz) % n_z) * 2 + c) for c in (0, 1) for dz in ring_order(n_z)
    ]
    dist = lambda d, n: min(d, n - d)
    moves = sorted(
        [(a, b) for a in range(n_y) for b in range(n_x) if (a, b) != (0, 0)],
        key=lambda m: -(dist(m[0], n_y) + dist(m[1], n_x)),
    )
    seq_peers = [((y_pos + a) % n_y) * n_x + (x_pos + b) % n_x for a, b in moves]

    barrier = pltpu.get_barrier_semaphore()
    for p in dp_peers:
        pl.semaphore_signal(barrier, inc=1, device_id=(p, me), device_id_type=MESH)
    for s in seq_peers:
        pl.semaphore_signal(barrier, inc=1, device_id=(dp, s), device_id_type=MESH)

    seg_copy.start()
    w_copy.start()

    shift = pack.bit_length() - 1
    dest_copy_in.wait()
    own_dest = dests[dp]
    tok_copy.wait()
    widened = tok[...].astype(F32)
    center = jnp.mean(widened, axis=-1, keepdims=True)
    spread = jnp.mean(jnp.square(widened - center), axis=-1, keepdims=True)
    normed = ((widened - center) * lax.rsqrt(spread + EPSILON)).astype(BF16)
    earlier = (iota((rows, rows), 0) < iota((rows, rows), 1)).astype(F32).astype(BF16)
    own_pack = lax.shift_right_logical(own_dest, shift)
    member = (iota((n_dp, rows), 0) == own_pack).astype(F32)
    rank = jnp.sum(member * dot(member.astype(BF16), earlier), axis=0, keepdims=True)
    slot = own_pack * slots + rank.astype(I32)
    pick = (iota((n_dp * slots, rows), 0) == slot).astype(F32).astype(BF16)
    sendx[...] = dot(pick, normed).astype(BF16)

    pl.semaphore_wait(barrier, len(dp_peers) + len(seq_peers))

    def dest_copy(p, slot_of):
        return pltpu.make_async_remote_copy(
            dests.at[dp], dests.at[slot_of], d_send, d_recv,
            device_id=(p, me), device_id_type=MESH,
        )

    def x_copy(p, slot_of, group):
        return pltpu.make_async_remote_copy(
            sendx.at[pl.ds(pl.multiple_of(p * slots, slots), slots)],
            recvx.at[pl.ds(pl.multiple_of(slot_of * slots, slots), slots)],
            x_send.at[group], x_recv,
            device_id=(p, me), device_id_type=MESH,
        )

    def seq_copy(src, dst, send, recv, s, slot_of):
        return pltpu.make_async_remote_copy(
            src.at[s], dst.at[slot_of], send, recv,
            device_id=(dp, s), device_id_type=MESH,
        )

    def wait_bytes(ref, count, sem):
        pltpu.make_async_copy(ref.at[pl.ds(0, count)], ref.at[pl.ds(0, count)], sem).wait()

    for p in dp_peers[0:4]:
        x_copy(p, dp, 0).start()
    for p in dp_peers[4:8]:
        x_copy(p, dp, 1).start()
    for p in dp_peers:
        dest_copy(p, dp).start()
    wait_bytes(sendx, 4 * slots, x_send.at[0])
    for p in dp_peers[8:12]:
        x_copy(p, dp, 2).start()
    wait_bytes(sendx, 4 * slots, x_send.at[1])
    for p in dp_peers[12:15]:
        x_copy(p, dp, 3).start()
    own = pl.ds(pl.multiple_of(dp * slots, slots), slots)
    recvx[own, :] = sendx[own, :]

    wait_bytes(dests, n_dp - 1, d_recv)
    all_dest = jnp.concatenate([dests[i] for i in range(n_dp)], axis=0)
    here = (lax.shift_right_logical(all_dest, shift) == dp).astype(F32)
    ranks = dot(here.astype(BF16), earlier).astype(I32)
    place = (all_dest & (pack - 1)) - me * rows
    pieces = []
    for i in range(n_dp):
        by_slot = jnp.where(
            iota((slots, rows), 0) == ranks[i : i + 1, :], here[i : i + 1, :], 0.0
        ).astype(BF16)
        by_place = (iota((rows, rows), 0) == place[i : i + 1, :]).astype(F32).astype(BF16)
        pieces.append(
            lax.dot_general(
                by_slot, by_place, (((1,), (1,)), ((), ())), preferred_element_type=F32
            )
        )
    unsort = jnp.concatenate(pieces, axis=0).T.astype(BF16)

    w_copy.wait()
    wait_bytes(recvx, (n_dp - 1) * slots, x_recv)
    x = dot(unsort, recvx[...]).astype(BF16)

    def project(begin, end):
        for c0 in range(begin, end, 256):
            c1 = min(c0 + 256, end)
            y_t[c0:c1, :] = dot(x, w[:, c0:c1]).T

    def kv_of(s):
        k = y_t[pl.ds(pl.multiple_of(width + s * HD, 8), HD), :]
        v = y_t[pl.ds(pl.multiple_of(2 * width + s * HD, 8), HD), :]
        return jnp.concatenate([k, v], axis=0).astype(BF16)

    pad = jnp.zeros((8, rows), F32)

    def q_of(s):
        q = y_t[pl.ds(pl.multiple_of(s * HD, 8), HD), :]
        return jnp.concatenate([q, pad], axis=0).astype(BF16)

    project(0, width)
    for s in seq_peers:
        sendq[s] = q_of(s)
        seq_copy(sendq, recvq, q_send, q_recv.at[me // pair], s, me).start()
    recvq[me] = q_of(me)
    project(width, 3 * width)
    for s in seq_peers:
        sendkv[s] = kv_of(s)
        seq_copy(sendkv, recvkv, kv_send, kv_recv.at[me], s, me).start()
    recvkv[me] = kv_of(me)

    def unpack(s):
        block = recvkv[s].astype(F32)
        k = jnp.concatenate([block[:HD], jnp.zeros((rows - HD, rows), F32)], axis=0)
        at = pl.ds(pl.multiple_of(s * rows, rows), rows)
        keys[at, :] = k.T.astype(BF16)
        values_t[:, at] = jnp.concatenate([block[HD:], pad], axis=0).astype(BF16)

    unpack(me)
    seg_copy.wait()
    for s in seq_peers:
        seq_copy(sendkv, recvkv, kv_send, kv_recv.at[s], s, s).wait_recv()
        unpack(s)

    factor = HD ** (-0.5) * math.log2(math.e)
    filler = jnp.zeros((keys.shape[1] - sendq.shape[1], UNIT), BF16)
    chunk = min(8, units)

    def spans(g):
        return slice(g * chunk * UNIT, (g + 1) * chunk * UNIT)

    def load(j, count):
        wait_bytes(recvq, count, q_recv.at[j])
        q = jnp.concatenate([recvq[j * pair + i] for i in range(pair)], axis=1)
        q_seg = seg[:, pl.ds(pl.multiple_of(j * UNIT, UNIT), UNIT)]
        same = [seg[:, u * UNIT : (u + 1) * UNIT] == q_seg for u in range(units)]
        return jnp.concatenate([q, filler], axis=0), same

    def score(g, q, same, peak, held):
        part = dot(keys[spans(g), :], q)
        held[spans(g), :] = part
        for i in range(chunk):
            top = jnp.max(part[i * UNIT : (i + 1) * UNIT], axis=0, keepdims=True)
            peak = jnp.where(same[g * chunk + i], jnp.maximum(peak, top), peak)
        return peak

    def mix(g, same, peak, held, totals, mixed):
        pieces = []
        for u in range(g * chunk, (g + 1) * chunk):
            level = jnp.where(same[u], peak, -MASKED_SCORE)
            piece = jnp.exp2((held[u * UNIT : (u + 1) * UNIT, :] - level) * factor)
            totals = totals + jnp.sum(piece.reshape(UNIT // 8, 8, UNIT), axis=0)
            pieces.append(piece.astype(BF16))
        weights = jnp.concatenate(pieces, axis=0)
        return totals, mixed + dot(values_t[:, spans(g)], weights)

    own_j = me // pair
    order = [(own_j + 1 + k) % units for k in range(units)]
    held = (scores_a, scores_b)
    floor = jnp.full((1, UNIT), MASKED_SCORE, F32)
    q, same = load(order[0], pair)
    peak = floor
    for g in range(units // chunk):
        peak = score(g, q, same, peak, held[0])
    for k in range(units):
        now_same, now_peak = same, peak
        last = k == units - 1
        if not last:
            q, same = load(order[k + 1], pair - 1 if k + 1 == units - 1 else pair)
            peak = floor
        totals = jnp.zeros((8, UNIT), F32)
        mixed = jnp.zeros((values_t.shape[0], UNIT), F32)
        for g in range(units // chunk):
            if not last:
                peak = score(g, q, same, peak, held[(k + 1) % 2])
            totals, mixed = mix(g, now_same, now_peak, held[k % 2], totals, mixed)
        result = (mixed / jnp.sum(totals, axis=0, keepdims=True)).astype(BF16)
        for i in range(pair):
            sendo[order[k] * pair + i] = result[:, i * rows : (i + 1) * rows]
        for i in range(1 if last else 0, pair):
            s = own_j * pair + (me + i) % pair if last else order[k] * pair + i
            seq_copy(sendo, heads_out, o_send, o_recv, s, me).start()
    own_copy = pltpu.make_async_copy(sendo.at[me], heads_out.at[me], in_sem.at[4])
    own_copy.start()

    wait_bytes(dests, n_dp - 1, d_send)
    wait_bytes(sendx, 4 * slots, x_send.at[2])
    wait_bytes(sendx, 3 * slots, x_send.at[3])
    wait_bytes(sendkv, n_seq - 1, kv_send)
    wait_bytes(sendq, n_seq - 1, q_send)
    own_copy.wait()
    wait_bytes(sendo, n_seq - 1, o_send)
    wait_bytes(heads_out, n_seq - 1, o_recv)


def assemble(heads, out, stacked):
    for h in range(heads.shape[0]):
        stacked[h * HD : (h + 1) * HD, :] = heads[h].astype(F32)[:HD]
    width = out.shape[2]
    for c0 in range(0, width, 128):
        c1 = min(c0 + 128, width)
        out[0, :, c0:c1] = stacked[c0:c1, :].T.astype(BF16)


def per_device(n_dp, n_seq, tok, dest, seg, projection):
    rows, width = tok.shape[1:]
    slots = 2 * rows // n_dp
    pack = n_seq * rows
    dma = pltpu.SemaphoreType.DMA
    vmem = pl.BlockSpec(memory_space=pltpu.VMEM)
    anywhere = pl.BlockSpec(memory_space=pl.ANY)
    heads = pl.pallas_call(
        functools.partial(kernel, n_dp, n_seq),
        out_shape=jax.ShapeDtypeStruct((n_seq, HD + 8, rows), BF16),
        in_specs=[anywhere] * 4,
        out_specs=anywhere,
        scratch_shapes=[
            pltpu.VMEM((rows, width), BF16),
            pltpu.VMEM(seg.shape, I32),
            pltpu.VMEM(projection.shape, BF16),
            pltpu.VMEM((n_dp * slots, width), BF16),
            pltpu.VMEM((n_dp * slots, width), BF16),
            pltpu.VMEM((n_dp, 1, rows), I32),
            pltpu.VMEM((3 * width, rows), F32),
            pltpu.VMEM((n_seq, 2 * HD, rows), BF16),
            pltpu.VMEM((n_seq, 2 * HD, rows), BF16),
            pltpu.VMEM((n_seq, HD + 8, rows), BF16),
            pltpu.VMEM((n_seq, HD + 8, rows), BF16),
            pltpu.VMEM((pack, 128), BF16),
            pltpu.VMEM((HD + 8, pack), BF16),
            pltpu.VMEM((pack, UNIT), F32),
            pltpu.VMEM((pack, UNIT), F32),
            pltpu.VMEM((n_seq, HD + 8, rows), BF16),
            dma((5,)),
            dma,
            dma,
            dma((4,)),
            dma,
            dma,
            dma((n_seq,)),
            dma,
            dma((pack // UNIT,)),
            dma,
            dma,
        ],
        compiler_params=pltpu.CompilerParams(
            collective_id=0, has_side_effects=True, vmem_limit_bytes=56 * 2**20
        ),
    )(tok, dest, seg, projection)
    return pl.pallas_call(
        assemble,
        out_shape=jax.ShapeDtypeStruct(tok.shape, BF16),
        in_specs=[vmem],
        out_specs=vmem,
        scratch_shapes=[pltpu.VMEM((width, rows), F32)],
        compiler_params=pltpu.CompilerParams(vmem_limit_bytes=32 * 2**20),
    )(heads)


def solution(mesh):
    placed = (P("dp", "seq", None), P("dp", "seq"), P("dp", None), P())
    return jax.shard_map(
        functools.partial(per_device, mesh.shape["dp"], mesh.shape["seq"]),
        mesh=mesh,
        in_specs=placed,
        out_specs=P("dp", "seq", None),
        check_vma=False,
    )
```
